32 devices in a mesh: seq: 8 (over z, y), head: 4 (over x, core).
Axes of the slice: x: 2, y: 2, z: 4, core: 2. Of those that a mesh axis runs over, the one named last changes fastest.
Arguments:
- block_input: float32 [2, 4096, 1024], P(None, 'seq'), may hold values from -6 to 6
- attn_gain: float32 [1024], replicated, may hold values from 0.5 to 1.5
- query_weight: bfloat16 [1024, 512], P(None, 'head'), may hold values from -0.1875 to 0.1875
- key_weight: bfloat16 [1024, 512], P(None, 'head'), may hold values from -0.1875 to 0.1875
- value_weight: bfloat16 [1024, 1024], P(None, 'head'), may hold values from -0.1875 to 0.1875
- gate_weight: bfloat16 [1024, 1024], P(None, 'head'), may hold values from -0.1875 to 0.1875
- decay_down: bfloat16 [1024, 16], replicated, may hold values from -0.1875 to 0.1875
- decay_up: bfloat16 [16, 512], P(None, 'head'), may hold values from -0.75 to 0.75
- decay_bias: float32 [512], P('head'), may hold values from -3 to 10
- query_conv: float32 [4, 512], P(None, 'head'), may hold values from -3 to 3
- key_conv: float32 [4, 512], P(None, 'head'), may hold values from -3 to 3
- value_conv: float32 [4, 1024], P(None, 'head'), may hold values from -3 to 3
- head_gain: float32 [256], replicated, may hold values from 0.5 to 1.5
- out_weight: bfloat16 [1024, 1024], P('head'), may hold values from -0.375 to 0.375
- ffn_gain: float32 [1024], replicated, may hold values from 0.5 to 1.5
- ffn_gate: bfloat16 [1024, 2816], P(None, 'head'), may hold values from -0.1875 to 0.1875
- ffn_up: bfloat16 [1024, 2816], P(None, 'head'), may hold values from -0.1875 to 0.1875
- ffn_down: bfloat16 [2816, 1024], P('head'), may hold values from -0.109375 to 0.109375
- out_grad: float32 [2, 4096, 1024], P(None, 'seq'), may hold values from -6 to 6
Outputs:
- block_output: float32 [2, 4096, 1024], P(None, 'seq')
- input_grad: float32 [2, 4096, 1024], P(None, 'seq')
- attn_gain_grad: float32 [1024], replicated
- query_weight_grad: float32 [1024, 512], P(None, 'head')
- key_weight_grad: float32 [1024, 512], P(None, 'head')
- value_weight_grad: float32 [1024, 1024], P(None, 'head')
- gate_weight_grad: float32 [1024, 1024], P(None, 'head')
- decay_down_grad: float32 [1024, 16], replicated
- decay_up_grad: float32 [16, 512], P(None, 'head')
- decay_bias_grad: float32 [512], P('head')
- query_conv_grad: float32 [4, 512], P(None, 'head')
- key_conv_grad: float32 [4, 512], P(None, 'head')
- value_conv_grad: float32 [4, 1024], P(None, 'head')
- head_gain_grad: float32 [256], replicated
- out_weight_grad: float32 [1024, 1024], P('head')
- ffn_gain_grad: float32 [1024], replicated
- ffn_gate_grad: float32 [1024, 2816], P(None, 'head')
- ffn_up_grad: float32 [1024, 2816], P(None, 'head')
- ffn_down_grad: float32 [2816, 1024], P('head')
The draws below stay inside these ranges and needn't reach their ends.
All inputs are finite; a program needn't handle non-finite values.
Results may differ from the reference program's by a relative error of at most 0.0075.
The reference program's roundings to bfloat16 on the way count: a program that leaves them out, or rounds other values in their place, can miss the bound.
Values sent between devices are 32-bit elements; how exact they have to be, the bound alone decides.
A program may use at most 192 MiB of HBM per device.

```python
import jax
import jax.numpy as jnp
from jax import lax

D = 1024
HEADS = 4
KEY = 128
VAL = 256
RANK = 16
FF = 2816
CONV = 4
GROUP = 64
SEQS = 2
LENGTH = 4096


def levels(rng, extent, cuts, least, top_value):
    factor_of, own = 1.0, jax.random.fold_in(rng, 6)
    for axis_at, parts in cuts:
        steps = jnp.exp(jax.random.uniform(jax.random.fold_in(own, axis_at), (parts,), jnp.float32, least / len(cuts), top_value / len(cuts)))
        factor_of = factor_of * jnp.repeat(steps, extent[axis_at] // parts).reshape([-1 if axis == axis_at else 1 for axis in range(len(extent))])
    return factor_of


def scatter_about(key, extent, scale, limit, cuts=(), held_as=jnp.bfloat16):
    factor_of = levels(key, extent, cuts, -0.22, 0.18) if cuts else 1.0
    array = jax.random.normal(key, extent, jnp.float32) * scale * factor_of
    return jnp.minimum(jnp.maximum(array, -limit), limit).astype(held_as)


def setup_inputs(seed: int = 0) -> dict:
    splits = jax.random.split(jax.random.key(seed), 20)
    return {
        "block_input": scatter_about(splits[0], (SEQS, LENGTH, D), 1.0, 6.0, ((1, 8),), jnp.float32),
        "attn_gain": jnp.clip(1.0 + 0.1 * jax.random.normal(splits[1], (D,), jnp.float32), 0.5, 1.5),
        "query_weight": scatter_about(splits[2], (D, HEADS * KEY), D ** -0.5, 0.1875, ((1, 4),)),
        "key_weight": scatter_about(splits[3], (D, HEADS * KEY), D ** -0.5, 0.1875, ((1, 4),)),
        "value_weight": scatter_about(splits[4], (D, HEADS * VAL), D ** -0.5, 0.1875, ((1, 4),)),
        "gate_weight": scatter_about(splits[5], (D, HEADS * VAL), D ** -0.5, 0.1875, ((1, 4),)),
        "decay_down": scatter_about(splits[6], (D, RANK), D ** -0.5, 0.1875),
        "decay_up": scatter_about(splits[7], (RANK, HEADS * KEY), (4 * RANK) ** -0.5, 0.75, ((1, 4),)),
        "decay_bias": jnp.clip(-3.0 + 13.0 * jax.random.uniform(splits[8], (HEADS * KEY,), jnp.float32) ** levels(splits[8], (HEADS * KEY,), ((0, 4),), -0.2, 0.2), -3.0, 10.0),
        "query_conv": scatter_about(splits[9], (CONV, HEADS * KEY), CONV ** -0.5, 3.0, ((1, 4),), jnp.float32),
        "key_conv": scatter_about(splits[10], (CONV, HEADS * KEY), CONV ** -0.5, 3.0, ((1, 4),), jnp.float32),
        "value_conv": scatter_about(splits[11], (CONV, HEADS * VAL), CONV ** -0.5, 3.0, ((1, 4),), jnp.float32),
        "head_gain": jnp.clip(1.0 + 0.1 * jax.random.normal(splits[12], (VAL,), jnp.float32), 0.5, 1.5),
        "out_weight": scatter_about(splits[13], (HEADS * VAL, D), (D // 4) ** -0.5, 0.375, ((0, 4),)),
        "ffn_gain": jnp.clip(1.0 + 0.1 * jax.random.normal(splits[14], (D,), jnp.float32), 0.5, 1.5),
        "ffn_gate": scatter_about(splits[15], (D, FF), D ** -0.5, 0.1875, ((1, 4),)),
        "ffn_up": scatter_about(splits[16], (D, FF), D ** -0.5, 0.1875, ((1, 4),)),
        "ffn_down": scatter_about(splits[17], (FF, D), FF ** -0.5, 0.109375, ((0, 4),)),
        "out_grad": scatter_about(splits[18], (SEQS, LENGTH, D), 1.0, 6.0, ((1, 8),), jnp.float32),
    }


EPS = 1e-06
HIGH = lax.Precision.HIGHEST

@jax.custom_vjp
def low(v):
    return lax.optimization_barrier(v.astype(jnp.bfloat16)).astype(jnp.float32)

@jax.custom_vjp
def low_back(v):
    return v

def low_keep(v):
    return (low(v), None)

def low_pass(kept, grad):
    return (grad,)

def back_keep(v):
    return (v, None)

def back_low(kept, grad):
    return (low(grad),)
low.defvjp(low_keep, low_pass)
low_back.defvjp(back_keep, back_low)

def matmul(left, right):
    return jnp.dot(left, right, precision=HIGH, preferred_element_type=jnp.float32)

def rms_scale(values):
    return lax.rsqrt(lax.optimization_barrier(jnp.mean(values * values, axis=-1, keepdims=True)) + EPS)

def causal_conv(raw_rows, taps_weight):
    taps = taps_weight.shape[0]
    padded = jnp.pad(raw_rows, ((0, 0), (taps - 1, 0), (0, 0)))
    count = raw_rows.shape[1]
    total = jnp.zeros_like(raw_rows)
    for offset in range(taps):
        total = total + taps_weight[offset] * padded[:, offset:offset + count]
    return jax.nn.silu(total)

def group_step(state, pieces):
    queries, key_rows, value_rows, decay_log = pieces
    inner = jnp.cumsum(decay_log, axis=1)
    count = inner.shape[1]
    lower = (jnp.arange(count)[:, None] >= jnp.arange(count)[None, :])[None, :, :, None]
    spread = inner[:, :, None, :] - inner[:, None, :, :]
    factors = jnp.exp(jnp.where(lower, spread, 0.0)) * lower.astype(jnp.float32)
    scores = jnp.einsum('btd,bsd,btsd->bts', queries, key_rows, factors, precision=HIGH)
    output = jnp.einsum('bts,bsv->btv', scores, value_rows, precision=HIGH)
    output = output + jnp.einsum('btk,bkv->btv', queries * jnp.exp(inner), state, precision=HIGH)
    last_row = inner[:, -1, :]
    carried = jnp.einsum('bsk,bsv->bkv', key_rows * jnp.exp(last_row[:, None, :] - inner), value_rows, precision=HIGH)
    state = jnp.exp(last_row)[:, :, None] * state + carried
    return (state, output)

def group_scan(queries, key_rows, value_rows, decay_log, state, group_len):
    count = queries.shape[1]

    def split(values):
        return jnp.moveaxis(values.reshape(values.shape[0], count // group_len, group_len, values.shape[2]), 1, 0)
    state, output = lax.scan(jax.checkpoint(group_step), state, (split(queries), split(key_rows), split(value_rows), split(decay_log)))
    output = jnp.moveaxis(output, 0, 1).reshape(queries.shape[0], count, value_rows.shape[2])
    return (output, state)

def forward(block_input, attn_gain, query_weight, key_weight, value_weight, gate_weight, decay_down, decay_up, decay_bias, query_conv, key_conv, value_conv, head_gain, out_weight, ffn_gain, ffn_gate, ffn_up, ffn_down):
    seq_count, seq_len, model_width = block_input.shape
    hidden_one = low(block_input * rms_scale(block_input) * attn_gain)
    query_raw = low_back(matmul(hidden_one, query_weight))
    key_raw = low_back(matmul(hidden_one, key_weight))
    value_raw = low_back(matmul(hidden_one, value_weight))
    gate_raw = low_back(matmul(hidden_one, gate_weight))
    decay_pre = matmul(matmul(hidden_one, decay_down), decay_up) + decay_bias
    decay_log = jax.nn.log_sigmoid(decay_pre) / 16.0
    queries = causal_conv(query_raw, query_conv) * KEY ** (-0.5)
    key_rows = causal_conv(key_raw, key_conv)
    value_rows = causal_conv(value_raw, value_conv)

    def heads_first(values):
        size = values.shape[2] // HEADS
        return values.reshape(seq_count, seq_len, HEADS, size).transpose(0, 2, 1, 3).reshape(seq_count * HEADS, seq_len, size)
    start = jnp.zeros((seq_count * HEADS, KEY, VAL), jnp.float32)
    mixed_rows, final_state = group_scan(heads_first(queries), heads_first(key_rows), heads_first(value_rows), heads_first(decay_log), start, GROUP)
    mixed_rows = mixed_rows.reshape(seq_count, HEADS, seq_len, VAL).transpose(0, 2, 1, 3)
    normed_gain = mixed_rows * rms_scale(mixed_rows) * head_gain
    gate_heads = jax.nn.silu(gate_raw.reshape(seq_count, seq_len, HEADS, VAL))
    gated_rows = low((normed_gain * gate_heads).reshape(seq_count, seq_len, HEADS * VAL))
    middle = block_input + low_back(matmul(gated_rows, out_weight))
    hidden_two = low(middle * rms_scale(middle) * ffn_gain)
    gate_rows = low_back(matmul(hidden_two, ffn_gate))
    up_rows = low_back(matmul(hidden_two, ffn_up))
    inner_rows = low(jax.nn.silu(gate_rows) * up_rows)
    return middle + low_back(matmul(inner_rows, ffn_down))

def reference(block_input, attn_gain, query_weight, key_weight, value_weight, gate_weight, decay_down, decay_up, decay_bias, query_conv, key_conv, value_conv, head_gain, out_weight, ffn_gain, ffn_gate, ffn_up, ffn_down, out_grad):
    params = [attn_gain, query_weight, key_weight, value_weight, gate_weight, decay_down, decay_up, decay_bias, query_conv, key_conv, value_conv, head_gain, out_weight, ffn_gain, ffn_gate, ffn_up, ffn_down]
    params = [item.astype(jnp.float32) for item in params]
    result, pull_back = jax.vjp(forward, block_input, *params)
    grads = pull_back(out_grad)
    return (result, grads[0], grads[1], grads[2], grads[3], grads[4], grads[5], grads[6], grads[7], grads[8], grads[9], grads[10], grads[11], grads[12], grads[13], grads[14], grads[15], grads[16], grads[17])
```

```python
import jax
import jax.numpy as jnp
import numpy as np
from jax import lax
from jax.experimental import pallas as pl
from jax.experimental.pallas import tpu as pltpu
from jax.sharding import PartitionSpec as P

EPS = 1e-06
HIGH = lax.Precision.HIGHEST


def shifted(value, axis, steps):
    count = lax.axis_size(axis)
    initial, last = (max(0, -steps), min(count, count - steps))
    return lax.ppermute(value, axis, [(source, source + steps) for source in range(initial, last)])


def rms_scale(values):
    return lax.rsqrt(jnp.mean(values * values, axis=-1, keepdims=True) + EPS)


def rms_back(grad_normed, normed, scale):
    return scale * (grad_normed - normed * jnp.mean(grad_normed * normed, axis=-1, keepdims=True))


def silu_slope(values):
    sigma = jax.nn.sigmoid(values)
    return sigma * (1.0 + values * (1.0 - sigma))


def half_dot(left, right):
    return jnp.dot(left, right, preferred_element_type=jnp.float32)


def half_outer(left, right):
    return lax.dot_general(
        left, right, (((0,), (0,)), ((), ())), preferred_element_type=jnp.float32
    )


def half_back(left, right):
    return lax.dot_general(
        left, right, (((1,), (1,)), ((), ())), preferred_element_type=jnp.float32
    )


def exact_dot(left, right):
    return jnp.dot(left, right, precision=HIGH, preferred_element_type=jnp.float32)


def exact_outer(left, right):
    return lax.dot_general(
        left, right, (((0,), (0,)), ((), ())), precision=HIGH, preferred_element_type=jnp.float32
    )


def exact_back(left, right):
    return lax.dot_general(
        left, right, (((1,), (1,)), ((), ())), precision=HIGH, preferred_element_type=jnp.float32
    )


def dot3(left, right, dims):
    left_high = left.astype(jnp.bfloat16)
    right_high = right.astype(jnp.bfloat16)
    left_low = (left - left_high.astype(jnp.float32)).astype(jnp.bfloat16)
    right_low = (right - right_high.astype(jnp.float32)).astype(jnp.bfloat16)

    def one(a, b):
        return lax.dot_general(a, b, (dims, ((), ())), preferred_element_type=jnp.float32)

    return one(left_high, right_high) + (one(left_high, right_low) + one(left_low, right_high))


PLAIN = ((1,), (0,))
BACK = ((1,), (1,))
OUTER = ((0,), (0,))


def sum_rows(zero_one, rows):
    first = rows.astype(jnp.bfloat16)
    rest = rows - first.astype(jnp.float32)
    second = rest.astype(jnp.bfloat16)
    third = (rest - second.astype(jnp.float32)).astype(jnp.bfloat16)

    def one(part):
        return jnp.dot(zero_one, part, preferred_element_type=jnp.float32)

    return one(first) + (one(second) + one(third))


def level_tables(size):
    place = np.arange(size)
    spans, masks = [], []
    half = size // 2
    while half >= 1:
        odd = (place // half) % 2 == 1
        edge = np.where(odd, (place // half) * half - 1, (place // half) * half + half - 1)
        column = place[None, :]
        forward = (column > edge[:, None]) & (column <= place[:, None])
        backward = (column > place[:, None]) & (column <= edge[:, None])
        spans.append(np.where(odd[:, None], forward, backward))
        same = (place[:, None] // (2 * half)) == (place[None, :] // (2 * half))
        masks.append(same & (odd[:, None] != odd[None, :]))
        half //= 2
    spans.append(place[None, :] <= place[:, None])
    spans.append(place[None, :] > place[:, None])
    return np.concatenate(spans).astype(np.float32), np.stack(masks).astype(np.float32)


def gla_forward_kernel(
    query, key, value, decay, spans, masks,
    out, query_decayed, scores_out, factors_out, states, prefix, last_state, last_decay,
    state, running,
):
    step = pl.program_id(0)
    seqs, size, width = query.shape
    levels = masks.shape[0]

    @pl.when(step == 0)
    def _():
        state[...] = jnp.zeros_like(state)
        running[...] = jnp.ones_like(running)

    row = lax.broadcasted_iota(jnp.int32, (size, size), 0)
    col = lax.broadcasted_iota(jnp.int32, (size, size), 1)
    row_wide = lax.broadcasted_iota(jnp.int32, (size, width), 0)
    for at in range(seqs):
        q, k, v = query[at], key[at], value[at]
        factors = jnp.exp(sum_rows(spans[...], decay[at]))
        factors_out[at, 0] = factors
        scores = jnp.where(row == col, jnp.sum(q * k, axis=1, keepdims=True), 0.0)
        for level in range(levels):
            half = size >> (level + 1)
            odd = (row_wide // half) % 2 == 1
            mixed = jnp.where(odd, q, k) * factors[level * size : (level + 1) * size]
            pairs = dot3(mixed, mixed, BACK) * masks[level]
            scores = scores + jnp.where(row > col, pairs, 0.0)
        scores_out[at, 0] = scores
        ahead = factors[levels * size : (levels + 1) * size]
        behind = factors[(levels + 1) * size :]
        whole = ahead[size - 1 : size]
        before = state[at]
        states[at, 0] = before
        prior = running[at, 0:1]
        prefix[at, 0] = running[at]
        query_ahead = q * ahead
        query_decayed[at] = query_ahead * prior
        out[at] = dot3(scores, v, PLAIN) + dot3(query_ahead, before, BACK)
        after = before * whole + dot3(v, k * behind, OUTER)
        state[at] = after
        running[at] = running[at] * whole
        last_state[at] = after
        last_decay[at] = running[at]


def gla_backward_kernel(
    query, key, value, grad, scores_in, factors_in, states, prefix, state_in, grad_last, masks, suffix,
    grad_query, grad_key, grad_value, grad_decay,
    grad_state,
):
    step = pl.program_id(0)
    seqs, size, width = query.shape
    levels = masks.shape[0]

    @pl.when(step == 0)
    def _():
        grad_state[...] = grad_last[...]

    row = lax.broadcasted_iota(jnp.int32, (size, size), 0)
    col = lax.broadcasted_iota(jnp.int32, (size, size), 1)
    row_wide = lax.broadcasted_iota(jnp.int32, (size, width), 0)
    for at in range(seqs):
        q, k, v, do = query[at], key[at], value[at], grad[at]
        factors = factors_in[at, 0]
        ahead = factors[levels * size : (levels + 1) * size]
        behind = factors[(levels + 1) * size :]
        whole = ahead[size - 1 : size]
        before = states[at, 0] + state_in[at] * prefix[at, 0, 0:1]
        after_grad = grad_state[at]
        key_behind = k * behind
        after = before * whole + dot3(v, key_behind, OUTER)
        dv = dot3(scores_in[at, 0], do, OUTER) + dot3(key_behind, after_grad, BACK)
        lower = dot3(do, v, BACK)
        both = jnp.where(row >= col, lower, dot3(v, do, BACK))
        diagonal = jnp.sum(do * v, axis=1, keepdims=True)
        dq = dot3(do, before, PLAIN) * ahead
        dk = dot3(v, after_grad, PLAIN) * behind
        for level in range(levels):
            half = size >> (level + 1)
            odd = (row_wide // half) % 2 == 1
            factor = factors[level * size : (level + 1) * size]
            mixed = jnp.where(odd, q, k) * factor
            back = dot3(both * masks[level], mixed, PLAIN) * factor
            dq = dq + jnp.where(odd, back, 0.0)
            dk = dk + jnp.where(odd, 0.0, back)
        carried = jnp.sum(after * after_grad, axis=0, keepdims=True)
        grad_decay[at] = sum_rows(suffix[...], q * dq - k * dk) + carried
        grad_query[at] = dq + diagonal * k
        grad_key[at] = dk + diagonal * q
        grad_value[at] = dv
        grad_state[at] = after_grad * whole + dot3(do, q * ahead, OUTER)


def chunk_of(count):
    size = 128
    while count % size:
        size //= 2
    return size


def gla_forward(query, key, value, decay):
    seqs, count, width = query.shape
    values = value.shape[2]
    size = chunk_of(count)
    chunks = count // size
    spans, masks = level_tables(size)
    tall = spans.shape[0]

    def rows(columns):
        return pl.BlockSpec((seqs, size, columns), lambda i: (0, i, 0))

    def whole(*shape):
        return pl.BlockSpec(shape, lambda i: (0,) * len(shape))

    def chunk(*shape):
        return pl.BlockSpec((seqs, 1) + shape, lambda i: (0, i, 0, 0))

    f32 = jnp.float32
    return pl.pallas_call(
        gla_forward_kernel,
        grid=(chunks,),
        in_specs=[rows(width), rows(width), rows(values), rows(width), whole(*spans.shape), whole(*masks.shape)],
        out_specs=[
            rows(values), rows(width), chunk(size, size), chunk(tall, width),
            chunk(values, width), chunk(8, width), whole(seqs, values, width), whole(seqs, 8, width),
        ],
        out_shape=[
            jax.ShapeDtypeStruct((seqs, count, values), f32),
            jax.ShapeDtypeStruct((seqs, count, width), f32),
            jax.ShapeDtypeStruct((seqs, chunks, size, size), f32),
            jax.ShapeDtypeStruct((seqs, chunks, tall, width), f32),
            jax.ShapeDtypeStruct((seqs, chunks, values, width), f32),
            jax.ShapeDtypeStruct((seqs, chunks, 8, width), f32),
            jax.ShapeDtypeStruct((seqs, values, width), f32),
            jax.ShapeDtypeStruct((seqs, 8, width), f32),
        ],
        scratch_shapes=[pltpu.VMEM((seqs, values, width), f32), pltpu.VMEM((seqs, 8, width), f32)],
        compiler_params=pltpu.CompilerParams(vmem_limit_bytes=48 * 1024 * 1024),
        name="gla_local",
    )(query, key, value, decay, jnp.asarray(spans, jnp.bfloat16), jnp.asarray(masks))


def gla_backward(query, key, value, grad, scores, factors, states, prefix, state_in, grad_last):
    seqs, count, width = query.shape
    values = value.shape[2]
    size = chunk_of(count)
    chunks = count // size
    spans, masks = level_tables(size)
    tall = spans.shape[0]
    suffix = np.triu(np.ones((size, size), np.float32))

    def rows(columns):
        return pl.BlockSpec((seqs, size, columns), lambda i: (0, chunks - 1 - i, 0))

    def whole(*shape):
        return pl.BlockSpec(shape, lambda i: (0,) * len(shape))

    def chunk(*shape):
        return pl.BlockSpec((seqs, 1) + shape, lambda i: (0, chunks - 1 - i, 0, 0))

    f32 = jnp.float32
    return pl.pallas_call(
        gla_backward_kernel,
        grid=(chunks,),
        in_specs=[
            rows(width), rows(width), rows(values), rows(values), chunk(size, size), chunk(tall, width),
            chunk(values, width), chunk(8, width), whole(seqs, values, width), whole(seqs, values, width),
            whole(*masks.shape), whole(*suffix.shape),
        ],
        out_specs=[rows(width), rows(width), rows(values), rows(width)],
        out_shape=[
            jax.ShapeDtypeStruct((seqs, count, width), f32),
            jax.ShapeDtypeStruct((seqs, count, width), f32),
            jax.ShapeDtypeStruct((seqs, count, values), f32),
            jax.ShapeDtypeStruct((seqs, count, width), f32),
        ],
        scratch_shapes=[pltpu.VMEM((seqs, values, width), f32)],
        compiler_params=pltpu.CompilerParams(vmem_limit_bytes=48 * 1024 * 1024),
        name="gla_back",
    )(query, key, value, grad, scores, factors, states, prefix, state_in, grad_last,
      jnp.asarray(masks), jnp.asarray(suffix, jnp.bfloat16))


def carried_in(decay, state, axis, reverse):
    count = lax.axis_size(axis)
    place = lax.axis_index(axis)
    ahead = count - 1 - place if reverse else place
    values = state.shape[1]
    gathered = lax.all_gather(jnp.concatenate([state, decay], axis=1), axis)
    total = jnp.zeros_like(state)

    def one(turn, total):
        source = count - 1 - turn if reverse else turn
        part = lax.dynamic_index_in_dim(gathered, source, 0, False)
        return jnp.where(turn < ahead, total * part[:, values : values + 1] + part[:, :values], total)

    if count <= 16:
        for turn in range(count - 1):
            total = one(turn, total)
        return total
    return lax.fori_loop(0, count - 1, one, total)


def shards(
    block_input,
    attn_gain,
    query_weight,
    key_weight,
    value_weight,
    gate_weight,
    decay_down,
    decay_up,
    decay_bias,
    query_conv,
    key_conv,
    value_conv,
    head_gain,
    out_weight,
    ffn_gain,
    ffn_gate,
    ffn_up,
    ffn_down,
    out_grad,
):
    seq_count, tok_rows, model_width = block_input.shape
    key_size = query_weight.shape[1]
    value_size = value_weight.shape[1]
    taps = query_conv.shape[0]
    row_count = seq_count * tok_rows
    inputs = block_input.reshape(row_count, model_width)
    scale_one = rms_scale(inputs)
    normed_one = inputs * scale_one
    hidden_one = (normed_one * attn_gain).astype(jnp.bfloat16)
    query_raw = half_dot(hidden_one, query_weight)
    key_raw = half_dot(hidden_one, key_weight)
    value_raw = half_dot(hidden_one, value_weight)
    gate_raw = half_dot(hidden_one, gate_weight)
    hidden_wide = hidden_one.astype(jnp.float32)
    down_wide = decay_down.astype(jnp.float32)
    up_wide = decay_up.astype(jnp.float32)
    rank_rows = exact_dot(hidden_wide, down_wide)
    decay_pre = exact_dot(rank_rows, up_wide) + decay_bias
    decay_log = (jax.nn.log_sigmoid(decay_pre) / 16.0).reshape(seq_count, tok_rows, key_size)
    conv_in = jnp.concatenate([query_raw, key_raw, value_raw], axis=1).reshape(
        seq_count, tok_rows, 2 * key_size + value_size
    )
    conv_weight = jnp.concatenate([query_conv, key_conv, value_conv], axis=1)
    edge_rows = shifted(conv_in[:, tok_rows - (taps - 1) :], "seq", 1)
    padded = jnp.concatenate([edge_rows, conv_in], axis=1)
    conv_pre = jnp.zeros_like(conv_in)
    for offset in range(taps):
        conv_pre = conv_pre + conv_weight[offset] * padded[:, offset : offset + tok_rows]
    conv_out = jax.nn.silu(conv_pre)
    factor = key_size ** (-0.5)
    queries = conv_out[:, :, :key_size] * factor
    key_rows = conv_out[:, :, key_size : 2 * key_size]
    value_rows = conv_out[:, :, 2 * key_size :]
    local_out, query_decayed, scores, factors, states, prefix, local_state, block_decay = gla_forward(
        queries, key_rows, value_rows, decay_log
    )
    state_in = carried_in(block_decay, local_state, "seq", False)
    mixed_rows = local_out + jnp.einsum("btk,bvk->btv", query_decayed, state_in, precision=HIGH)
    mixed_rows = mixed_rows.reshape(row_count, value_size)
    head_scale = rms_scale(mixed_rows)
    head_normed = mixed_rows * head_scale
    normed_gain = head_normed * head_gain
    gate_act = jax.nn.silu(gate_raw)
    gated_rows = (normed_gain * gate_act).astype(jnp.bfloat16)
    mixer_out = lax.psum(half_dot(gated_rows, out_weight), "head")
    middle = inputs + mixer_out
    scale_two = rms_scale(middle)
    normed_two = middle * scale_two
    hidden_two = (normed_two * ffn_gain).astype(jnp.bfloat16)
    gate_rows = half_dot(hidden_two, ffn_gate)
    up_rows = half_dot(hidden_two, ffn_up)
    inner_rows = (jax.nn.silu(gate_rows) * up_rows).astype(jnp.bfloat16)
    ffn_out = lax.psum(half_dot(inner_rows, ffn_down), "head")
    block_output = (middle + ffn_out).reshape(seq_count, tok_rows, model_width)
    grad_rows = out_grad.reshape(row_count, model_width)
    grad_ffn = grad_rows.astype(jnp.bfloat16)
    ffn_down_grad = half_outer(inner_rows, grad_ffn)
    grad_inner = half_back(grad_ffn, ffn_down)
    grad_up = (grad_inner * jax.nn.silu(gate_rows)).astype(jnp.bfloat16)
    grad_gate = (grad_inner * up_rows * silu_slope(gate_rows)).astype(jnp.bfloat16)
    ffn_gate_grad = half_outer(hidden_two, grad_gate)
    ffn_up_grad = half_outer(hidden_two, grad_up)
    grad_hidden_two = lax.psum(half_back(grad_gate, ffn_gate) + half_back(grad_up, ffn_up), "head")
    ffn_gain_grad = jnp.sum(grad_hidden_two * normed_two, axis=0)
    grad_middle = grad_rows + rms_back(grad_hidden_two * ffn_gain, normed_two, scale_two)
    grad_mixer = grad_middle.astype(jnp.bfloat16)
    out_weight_grad = half_outer(gated_rows, grad_mixer)
    grad_gated = half_back(grad_mixer, out_weight)
    grad_normed = grad_gated * gate_act
    grad_gate_raw = (grad_gated * normed_gain * silu_slope(gate_raw)).astype(jnp.bfloat16)
    head_gain_part = jnp.sum(grad_normed * head_normed, axis=0)
    grad_mixed = rms_back(grad_normed * head_gain, head_normed, head_scale).reshape(
        seq_count, tok_rows, value_size
    )
    state_pull = jnp.einsum("btk,btv->bvk", query_decayed, grad_mixed, precision=HIGH)
    grad_state_out = carried_in(block_decay, state_pull, "seq", True)
    grad_queries, grad_keys, grad_values, grad_decay = gla_backward(
        queries, key_rows, value_rows, grad_mixed, scores, factors, states, prefix, state_in, grad_state_out
    )
    grad_conv_out = jnp.concatenate([grad_queries * factor, grad_keys, grad_values], axis=2)
    grad_conv_pre = grad_conv_out * silu_slope(conv_pre)
    grad_padded = jnp.zeros_like(padded)
    tap_grads = []
    for offset in range(taps):
        grad_padded = grad_padded + jnp.pad(
            conv_weight[offset] * grad_conv_pre, ((0, 0), (offset, taps - 1 - offset), (0, 0))
        )
        tap_grads.append(
            jnp.sum(padded[:, offset : offset + tok_rows] * grad_conv_pre, axis=(0, 1))
        )
    conv_grad = jnp.stack(tap_grads)
    edge_back = shifted(grad_padded[:, : taps - 1], "seq", -1)
    grad_conv_in = grad_padded[:, taps - 1 :] + jnp.pad(
        edge_back, ((0, 0), (tok_rows - taps + 1, 0), (0, 0))
    )
    grad_in_rows = grad_conv_in.reshape(row_count, 2 * key_size + value_size).astype(jnp.bfloat16)
    grad_query_raw = grad_in_rows[:, :key_size]
    grad_key_raw = grad_in_rows[:, key_size : 2 * key_size]
    grad_value_raw = grad_in_rows[:, 2 * key_size :]
    grad_pre = grad_decay.reshape(row_count, key_size) / 16.0 * jax.nn.sigmoid(-decay_pre)
    decay_bias_grad = jnp.sum(grad_pre, axis=0)
    decay_up_grad = exact_outer(rank_rows, grad_pre)
    grad_rank = exact_back(grad_pre, up_wide)
    decay_down_part = exact_outer(hidden_wide, grad_rank)
    query_weight_grad = half_outer(hidden_one, grad_query_raw)
    key_weight_grad = half_outer(hidden_one, grad_key_raw)
    value_weight_grad = half_outer(hidden_one, grad_value_raw)
    gate_weight_grad = half_outer(hidden_one, grad_gate_raw)
    hidden_part = half_back(grad_query_raw, query_weight) + half_back(grad_key_raw, key_weight)
    hidden_part = (
        hidden_part
        + half_back(grad_value_raw, value_weight)
        + half_back(grad_gate_raw, gate_weight)
    )
    hidden_part = hidden_part + exact_back(grad_rank, down_wide)
    grad_hidden_one = lax.psum(hidden_part, "head")
    attn_gain_grad = jnp.sum(grad_hidden_one * normed_one, axis=0)
    input_grad = (
        grad_middle + rms_back(grad_hidden_one * attn_gain, normed_one, scale_one)
    ).reshape(seq_count, tok_rows, model_width)
    decay_down_grad, head_gain_grad = lax.psum((decay_down_part, head_gain_part), ("seq", "head"))
    (
        attn_gain_grad,
        query_weight_grad,
        key_weight_grad,
        value_weight_grad,
        gate_weight_grad,
        decay_up_grad,
        decay_bias_grad,
        conv_grad,
        out_weight_grad,
        ffn_gain_grad,
        ffn_gate_grad,
        ffn_up_grad,
        ffn_down_grad,
    ) = lax.psum(
        (
            attn_gain_grad,
            query_weight_grad,
            key_weight_grad,
            value_weight_grad,
            gate_weight_grad,
            decay_up_grad,
            decay_bias_grad,
            conv_grad,
            out_weight_grad,
            ffn_gain_grad,
            ffn_gate_grad,
            ffn_up_grad,
            ffn_down_grad,
        ),
        "seq",
    )
    query_conv_grad = conv_grad[:, :key_size]
    key_conv_grad = conv_grad[:, key_size : 2 * key_size]
    value_conv_grad = conv_grad[:, 2 * key_size :]
    return (
        block_output,
        input_grad,
        attn_gain_grad,
        query_weight_grad,
        key_weight_grad,
        value_weight_grad,
        gate_weight_grad,
        decay_down_grad,
        decay_up_grad,
        decay_bias_grad,
        query_conv_grad,
        key_conv_grad,
        value_conv_grad,
        head_gain_grad,
        out_weight_grad,
        ffn_gain_grad,
        ffn_gate_grad,
        ffn_up_grad,
        ffn_down_grad,
    )


def solution(mesh):
    in_specs = (
        P(None, "seq", None),
        P(),
        P(None, "head"),
        P(None, "head"),
        P(None, "head"),
        P(None, "head"),
        P(),
        P(None, "head"),
        P("head"),
        P(None, "head"),
        P(None, "head"),
        P(None, "head"),
        P(),
        P("head", None),
        P(),
        P(None, "head"),
        P(None, "head"),
        P("head", None),
        P(None, "seq", None),
    )
    out_specs = (
        P(None, "seq", None),
        P(None, "seq", None),
        P(),
        P(None, "head"),
        P(None, "head"),
        P(None, "head"),
        P(None, "head"),
        P(),
        P(None, "head"),
        P("head"),
        P(None, "head"),
        P(None, "head"),
        P(None, "head"),
        P(),
        P("head", None),
        P(),
        P(None, "head"),
        P(None, "head"),
        P("head", None),
    )
    return jax.shard_map(shards, mesh=mesh, in_specs=in_specs, out_specs=out_specs, check_vma=False)
```

```python
import functools

import jax
import jax.numpy as jnp
import numpy as np
from jax import lax
from jax.experimental import pallas as pl
from jax.experimental.pallas import tpu as pltpu
from jax.sharding import PartitionSpec as P

EPS = 1e-06
HIGH = lax.Precision.HIGHEST


def shifted(value, axis, steps):
    count = lax.axis_size(axis)
    initial, last = (max(0, -steps), min(count, count - steps))
    return lax.ppermute(value, axis, [(source, source + steps) for source in range(initial, last)])


def rms_scale(values):
    return lax.rsqrt(jnp.mean(values * values, axis=-1, keepdims=True) + EPS)


def rms_back(grad_normed, normed, scale):
    return scale * (grad_normed - normed * jnp.mean(grad_normed * normed, axis=-1, keepdims=True))


def silu_slope(values):
    sigma = jax.nn.sigmoid(values)
    return sigma * (1.0 + values * (1.0 - sigma))


def half_dot(left, right):
    return jnp.dot(left, right, preferred_element_type=jnp.float32)


def half_outer(left, right):
    return lax.dot_general(
        left, right, (((0,), (0,)), ((), ())), preferred_element_type=jnp.float32
    )


def half_back(left, right):
    return lax.dot_general(
        left, right, (((1,), (1,)), ((), ())), preferred_element_type=jnp.float32
    )


def exact_dot(left, right):
    return jnp.dot(left, right, precision=HIGH, preferred_element_type=jnp.float32)


def exact_outer(left, right):
    return lax.dot_general(
        left, right, (((0,), (0,)), ((), ())), precision=HIGH, preferred_element_type=jnp.float32
    )


def exact_back(left, right):
    return lax.dot_general(
        left, right, (((1,), (1,)), ((), ())), precision=HIGH, preferred_element_type=jnp.float32
    )


def dot3(left, right, dims):
    left_high = left.astype(jnp.bfloat16)
    right_high = right.astype(jnp.bfloat16)
    left_low = (left - left_high.astype(jnp.float32)).astype(jnp.bfloat16)
    right_low = (right - right_high.astype(jnp.float32)).astype(jnp.bfloat16)

    def one(a, b):
        return lax.dot_general(a, b, (dims, ((), ())), preferred_element_type=jnp.float32)

    return one(left_high, right_high) + (one(left_high, right_low) + one(left_low, right_high))


PLAIN = ((1,), (0,))
BACK = ((1,), (1,))
OUTER = ((0,), (0,))


def sum_rows(zero_one, rows):
    first = rows.astype(jnp.bfloat16)
    rest = rows - first.astype(jnp.float32)
    second = rest.astype(jnp.bfloat16)
    third = (rest - second.astype(jnp.float32)).astype(jnp.bfloat16)

    def one(part):
        return jnp.dot(zero_one, part, preferred_element_type=jnp.float32)

    return one(first) + (one(second) + one(third))


def level_tables(size):
    place = np.arange(size)
    spans, masks = [], []
    half = size // 2
    while half >= 1:
        odd = (place // half) % 2 == 1
        edge = np.where(odd, (place // half) * half - 1, (place // half) * half + half - 1)
        column = place[None, :]
        forward = (column > edge[:, None]) & (column <= place[:, None])
        backward = (column > place[:, None]) & (column <= edge[:, None])
        spans.append(np.where(odd[:, None], forward, backward))
        same = (place[:, None] // (2 * half)) == (place[None, :] // (2 * half))
        masks.append(same & (odd[:, None] != odd[None, :]))
        half //= 2
    spans.append(place[None, :] <= place[:, None])
    spans.append(place[None, :] > place[:, None])
    return np.concatenate(spans).astype(np.float32), np.stack(masks).astype(np.float32)


def gla_forward_kernel(
    query, key, value, decay, spans, masks,
    out, query_decayed, scores_out, factors_out, states, prefix, last_state, last_decay,
    state, running,
):
    step = pl.program_id(0)
    seqs, size, width = query.shape
    levels = masks.shape[0]

    @pl.when(step == 0)
    def _():
        state[...] = jnp.zeros_like(state)
        running[...] = jnp.ones_like(running)

    row = lax.broadcasted_iota(jnp.int32, (size, size), 0)
    col = lax.broadcasted_iota(jnp.int32, (size, size), 1)
    row_wide = lax.broadcasted_iota(jnp.int32, (size, width), 0)
    for at in range(seqs):
        q, k, v = query[at], key[at], value[at]
        factors = jnp.exp(sum_rows(spans[...], decay[at]))
        factors_out[at, 0] = factors
        scores = jnp.where(row == col, jnp.sum(q * k, axis=1, keepdims=True), 0.0)
        for level in range(levels):
            half = size >> (level + 1)
            odd = (row_wide // half) % 2 == 1
            mixed = jnp.where(odd, q, k) * factors[level * size : (level + 1) * size]
            pairs = dot3(mixed, mixed, BACK) * masks[level]
            scores = scores + jnp.where(row > col, pairs, 0.0)
        scores_out[at, 0] = scores
        ahead = factors[levels * size : (levels + 1) * size]
        behind = factors[(levels + 1) * size :]
        whole = ahead[size - 1 : size]
        before = state[at]
        states[at, 0] = before
        prior = running[at, 0:1]
        prefix[at, 0] = running[at]
        query_ahead = q * ahead
        query_decayed[at] = query_ahead * prior
        out[at] = dot3(scores, v, PLAIN) + dot3(query_ahead, before, BACK)
        after = before * whole + dot3(v, k * behind, OUTER)
        state[at] = after
        running[at] = running[at] * whole
        last_state[at] = after
        last_decay[at] = running[at]


def gla_backward_kernel(
    query, key, value, grad, scores_in, factors_in, states, prefix, state_in, grad_last, masks, suffix,
    grad_query, grad_key, grad_value, grad_decay,
    grad_state,
):
    step = pl.program_id(0)
    seqs, size, width = query.shape
    levels = masks.shape[0]

    @pl.when(step == 0)
    def _():
        grad_state[...] = grad_last[...]

    row = lax.broadcasted_iota(jnp.int32, (size, size), 0)
    col = lax.broadcasted_iota(jnp.int32, (size, size), 1)
    row_wide = lax.broadcasted_iota(jnp.int32, (size, width), 0)
    for at in range(seqs):
        q, k, v, do = query[at], key[at], value[at], grad[at]
        factors = factors_in[at, 0]
        ahead = factors[levels * size : (levels + 1) * size]
        behind = factors[(levels + 1) * size :]
        whole = ahead[size - 1 : size]
        before = states[at, 0] + state_in[at] * prefix[at, 0, 0:1]
        after_grad = grad_state[at]
        key_behind = k * behind
        after = before * whole + dot3(v, key_behind, OUTER)
        dv = dot3(scores_in[at, 0], do, OUTER) + dot3(key_behind, after_grad, BACK)
        lower = dot3(do, v, BACK)
        both = jnp.where(row >= col, lower, dot3(v, do, BACK))
        diagonal = jnp.sum(do * v, axis=1, keepdims=True)
        dq = dot3(do, before, PLAIN) * ahead
        dk = dot3(v, after_grad, PLAIN) * behind
        for level in range(levels):
            half = size >> (level + 1)
            odd = (row_wide // half) % 2 == 1
            factor = factors[level * size : (level + 1) * size]
            mixed = jnp.where(odd, q, k) * factor
            back = dot3(both * masks[level], mixed, PLAIN) * factor
            dq = dq + jnp.where(odd, back, 0.0)
            dk = dk + jnp.where(odd, 0.0, back)
        carried = jnp.sum(after * after_grad, axis=0, keepdims=True)
        grad_decay[at] = sum_rows(suffix[...], q * dq - k * dk) + carried
        grad_query[at] = dq + diagonal * k
        grad_key[at] = dk + diagonal * q
        grad_value[at] = dv
        grad_state[at] = after_grad * whole + dot3(do, q * ahead, OUTER)


def chunk_of(count):
    size = 128
    while count % size:
        size //= 2
    return size


def gla_forward(query, key, value, decay):
    seqs, count, width = query.shape
    values = value.shape[2]
    size = chunk_of(count)
    chunks = count // size
    spans, masks = level_tables(size)
    tall = spans.shape[0]

    def rows(columns):
        return pl.BlockSpec((seqs, size, columns), lambda i: (0, i, 0))

    def whole(*shape):
        return pl.BlockSpec(shape, lambda i: (0,) * len(shape))

    def chunk(*shape):
        return pl.BlockSpec((seqs, 1) + shape, lambda i: (0, i, 0, 0))

    f32 = jnp.float32
    return pl.pallas_call(
        gla_forward_kernel,
        grid=(chunks,),
        in_specs=[rows(width), rows(width), rows(values), rows(width), whole(*spans.shape), whole(*masks.shape)],
        out_specs=[
            rows(values), rows(width), chunk(size, size), chunk(tall, width),
            chunk(values, width), chunk(8, width), whole(seqs, values, width), whole(seqs, 8, width),
        ],
        out_shape=[
            jax.ShapeDtypeStruct((seqs, count, values), f32),
            jax.ShapeDtypeStruct((seqs, count, width), f32),
            jax.ShapeDtypeStruct((seqs, chunks, size, size), f32),
            jax.ShapeDtypeStruct((seqs, chunks, tall, width), f32),
            jax.ShapeDtypeStruct((seqs, chunks, values, width), f32),
            jax.ShapeDtypeStruct((seqs, chunks, 8, width), f32),
            jax.ShapeDtypeStruct((seqs, values, width), f32),
            jax.ShapeDtypeStruct((seqs, 8, width), f32),
        ],
        scratch_shapes=[pltpu.VMEM((seqs, values, width), f32), pltpu.VMEM((seqs, 8, width), f32)],
        compiler_params=pltpu.CompilerParams(vmem_limit_bytes=48 * 1024 * 1024),
        name="gla_local",
    )(query, key, value, decay, jnp.asarray(spans, jnp.bfloat16), jnp.asarray(masks))


def gla_backward(query, key, value, grad, scores, factors, states, prefix, state_in, grad_last):
    seqs, count, width = query.shape
    values = value.shape[2]
    size = chunk_of(count)
    chunks = count // size
    spans, masks = level_tables(size)
    tall = spans.shape[0]
    suffix = np.triu(np.ones((size, size), np.float32))

    def rows(columns):
        return pl.BlockSpec((seqs, size, columns), lambda i: (0, chunks - 1 - i, 0))

    def whole(*shape):
        return pl.BlockSpec(shape, lambda i: (0,) * len(shape))

    def chunk(*shape):
        return pl.BlockSpec((seqs, 1) + shape, lambda i: (0, chunks - 1 - i, 0, 0))

    f32 = jnp.float32
    return pl.pallas_call(
        gla_backward_kernel,
        grid=(chunks,),
        in_specs=[
            rows(width), rows(width), rows(values), rows(values), chunk(size, size), chunk(tall, width),
            chunk(values, width), chunk(8, width), whole(seqs, values, width), whole(seqs, values, width),
            whole(*masks.shape), whole(*suffix.shape),
        ],
        out_specs=[rows(width), rows(width), rows(values), rows(width)],
        out_shape=[
            jax.ShapeDtypeStruct((seqs, count, width), f32),
            jax.ShapeDtypeStruct((seqs, count, width), f32),
            jax.ShapeDtypeStruct((seqs, count, values), f32),
            jax.ShapeDtypeStruct((seqs, count, width), f32),
        ],
        scratch_shapes=[pltpu.VMEM((seqs, values, width), f32)],
        compiler_params=pltpu.CompilerParams(vmem_limit_bytes=48 * 1024 * 1024),
        name="gla_back",
    )(query, key, value, grad, scores, factors, states, prefix, state_in, grad_last,
      jnp.asarray(masks), jnp.asarray(suffix, jnp.bfloat16))


MESH = pl.DeviceIdType.MESH


def greet(axis, partners):
    barrier = pltpu.get_barrier_semaphore()
    for partner in partners:
        pl.semaphore_signal(barrier, inc=1, device_id={axis: partner}, device_id_type=MESH)
    pl.semaphore_wait(barrier, len(partners))


def prefix_kernel(axis, reverse, block, out, total, received, send_sem, recv_sem):
    steps, seqs, tall, width = total.shape
    values = tall - 8
    me = lax.axis_index(axis)
    uppers = [(me // (1 << step)) % 2 for step in range(steps)]
    partners = [me + (1 << step) * (1 - 2 * upper) for step, upper in enumerate(uppers)]
    greet(axis, partners)
    total[0] = block[...]
    out[...] = jnp.zeros_like(out)
    passed = jnp.ones((seqs, 1, width), jnp.float32)
    for step in range(steps):
        copy = pltpu.make_async_remote_copy(
            src_ref=total.at[step],
            dst_ref=received.at[step],
            send_sem=send_sem.at[step],
            recv_sem=recv_sem.at[step],
            device_id={axis: partners[step]},
            device_id_type=MESH,
        )
        copy.start()
        copy.wait()
        later = uppers[step] == (0 if reverse else 1)
        theirs = received[step, :, :values]
        their_decay = received[step, :, values:]
        out[...] = jnp.where(later, theirs * passed + out[...], out[...])
        passed = jnp.where(later, their_decay[:, 0:1] * passed, passed)
        if step + 1 < steps:
            mine = total[step, :, :values]
            my_decay = total[step, :, values:]
            total[step + 1, :, :values] = jnp.where(
                later, theirs * my_decay[:, 0:1] + mine, mine * their_decay[:, 0:1] + theirs
            )
            total[step + 1, :, values:] = my_decay * their_decay


def carried_in(decay, state, axis, reverse, call_id):
    count = lax.axis_size(axis)
    steps = count.bit_length() - 1
    assert count == 1 << steps
    block = jnp.concatenate([state, decay], axis=1)
    slots = pltpu.VMEM((steps,) + block.shape, jnp.float32)
    return pl.pallas_call(
        functools.partial(prefix_kernel, axis, reverse),
        out_shape=jax.ShapeDtypeStruct(state.shape, jnp.float32),
        in_specs=[pl.BlockSpec(memory_space=pltpu.VMEM)],
        out_specs=pl.BlockSpec(memory_space=pltpu.VMEM),
        scratch_shapes=[slots, slots, pltpu.SemaphoreType.DMA((steps,)), pltpu.SemaphoreType.DMA((steps,))],
        compiler_params=pltpu.CompilerParams(
            collective_id=call_id, has_side_effects=True, vmem_limit_bytes=32 * 1024 * 1024
        ),
        name="state_prefix",
    )(block)


def sum_kernel(axis, terms, out, partial, from_near, from_far, send_sem, recv_sem):
    pieces = terms.shape[0]
    me = lax.axis_index(axis)
    low, high = me % 2, me // 2
    near = me + 1 - 2 * low
    far = me + 2 - 4 * high
    mine = 2 * low + high
    other = 2 * low + 1 - high
    greet(axis, [near, far])

    def copy(kind, piece, source, target, device):
        return pltpu.make_async_remote_copy(
            src_ref=source,
            dst_ref=target,
            send_sem=send_sem.at[kind, piece],
            recv_sem=recv_sem.at[kind, piece],
            device_id={axis: device},
            device_id_type=MESH,
        )

    def halves(piece):
        return copy(0, piece, terms.at[piece, pl.ds(2 - 2 * low, 2)], from_near.at[piece], near)

    def quarters(piece):
        return copy(1, piece, partial.at[piece, 1 - high], from_far.at[piece], far)

    def back_far(piece):
        return copy(2, piece, out.at[piece, mine], out.at[piece, mine], far)

    def back_near(piece):
        return copy(3, piece, out.at[piece, mine], out.at[piece, mine], near)

    def pass_near(piece):
        return copy(4, piece, out.at[piece, other], out.at[piece, other], near)

    for piece in range(pieces):
        halves(piece).start()
    for piece in range(pieces):
        halves(piece).wait_recv()
        partial[piece] = terms[piece, pl.ds(2 * low, 2)] + from_near[piece]
        quarters(piece).start()
    for piece in range(pieces):
        quarters(piece).wait_recv()
        out[piece, mine] = partial[piece, high] + from_far[piece]
        back_far(piece).start()
        back_near(piece).start()
    for piece in range(pieces):
        back_far(piece).wait_recv()
        pass_near(piece).start()
    for piece in range(pieces):
        back_near(piece).wait_recv()
        pass_near(piece).wait_recv()
        for made in (halves, quarters, back_far, back_near, pass_near):
            made(piece).wait_send()


def head_sum(terms, axis, call_id):
    rows, columns = terms.shape
    if lax.axis_size(axis) != 4 or rows % 32:
        return lax.psum(terms, axis)
    pieces = next(count for count in (4, 5, 3, 2, 1) if rows % (32 * count) == 0)
    deep = rows // (4 * pieces)
    f32 = jnp.float32
    out = pl.pallas_call(
        functools.partial(sum_kernel, axis),
        out_shape=jax.ShapeDtypeStruct((pieces, 4, deep, columns), f32),
        in_specs=[pl.BlockSpec(memory_space=pltpu.VMEM)],
        out_specs=pl.BlockSpec(memory_space=pltpu.VMEM),
        scratch_shapes=[
            pltpu.VMEM((pieces, 2, deep, columns), f32),
            pltpu.VMEM((pieces, 2, deep, columns), f32),
            pltpu.VMEM((pieces, deep, columns), f32),
            pltpu.SemaphoreType.DMA((5, pieces)),
            pltpu.SemaphoreType.DMA((5, pieces)),
        ],
        compiler_params=pltpu.CompilerParams(
            collective_id=call_id, has_side_effects=True, vmem_limit_bytes=48 * 1024 * 1024
        ),
        name="head_sum",
    )(terms.reshape(pieces, 4, deep, columns))
    return out.reshape(rows, columns)


def shards(
    block_input,
    attn_gain,
    query_weight,
    key_weight,
    value_weight,
    gate_weight,
    decay_down,
    decay_up,
    decay_bias,
    query_conv,
    key_conv,
    value_conv,
    head_gain,
    out_weight,
    ffn_gain,
    ffn_gate,
    ffn_up,
    ffn_down,
    out_grad,
):
    seq_count, tok_rows, model_width = block_input.shape
    key_size = query_weight.shape[1]
    value_size = value_weight.shape[1]
    taps = query_conv.shape[0]
    row_count = seq_count * tok_rows
    inputs = block_input.reshape(row_count, model_width)
    scale_one = rms_scale(inputs)
    normed_one = inputs * scale_one
    hidden_one = (normed_one * attn_gain).astype(jnp.bfloat16)
    query_raw = half_dot(hidden_one, query_weight)
    key_raw = half_dot(hidden_one, key_weight)
    value_raw = half_dot(hidden_one, value_weight)
    gate_raw = half_dot(hidden_one, gate_weight)
    hidden_wide = hidden_one.astype(jnp.float32)
    down_wide = decay_down.astype(jnp.float32)
    up_wide = decay_up.astype(jnp.float32)
    rank_rows = exact_dot(hidden_wide, down_wide)
    decay_pre = exact_dot(rank_rows, up_wide) + decay_bias
    decay_log = (jax.nn.log_sigmoid(decay_pre) / 16.0).reshape(seq_count, tok_rows, key_size)
    conv_in = jnp.concatenate([query_raw, key_raw, value_raw], axis=1).reshape(
        seq_count, tok_rows, 2 * key_size + value_size
    )
    conv_weight = jnp.concatenate([query_conv, key_conv, value_conv], axis=1)
    edge_rows = shifted(conv_in[:, tok_rows - (taps - 1) :], "seq", 1)
    padded = jnp.concatenate([edge_rows, conv_in], axis=1)
    conv_pre = jnp.zeros_like(conv_in)
    for offset in range(taps):
        conv_pre = conv_pre + conv_weight[offset] * padded[:, offset : offset + tok_rows]
    conv_out = jax.nn.silu(conv_pre)
    factor = key_size ** (-0.5)
    queries = conv_out[:, :, :key_size] * factor
    key_rows = conv_out[:, :, key_size : 2 * key_size]
    value_rows = conv_out[:, :, 2 * key_size :]
    local_out, query_decayed, scores, factors, states, prefix, local_state, block_decay = gla_forward(
        queries, key_rows, value_rows, decay_log
    )
    state_in = carried_in(block_decay, local_state, "seq", False, 0)
    mixed_rows = local_out + jnp.einsum("btk,bvk->btv", query_decayed, state_in, precision=HIGH)
    mixed_rows = mixed_rows.reshape(row_count, value_size)
    head_scale = rms_scale(mixed_rows)
    head_normed = mixed_rows * head_scale
    normed_gain = head_normed * head_gain
    gate_act = jax.nn.silu(gate_raw)
    gated_rows = (normed_gain * gate_act).astype(jnp.bfloat16)
    mixer_out = head_sum(half_dot(gated_rows, out_weight), "head", 2)
    middle = inputs + mixer_out
    scale_two = rms_scale(middle)
    normed_two = middle * scale_two
    hidden_two = (normed_two * ffn_gain).astype(jnp.bfloat16)
    gate_rows = half_dot(hidden_two, ffn_gate)
    up_rows = half_dot(hidden_two, ffn_up)
    inner_rows = (jax.nn.silu(gate_rows) * up_rows).astype(jnp.bfloat16)
    ffn_part = half_dot(inner_rows, ffn_down)
    grad_rows = out_grad.reshape(row_count, model_width)
    grad_ffn = grad_rows.astype(jnp.bfloat16)
    ffn_down_grad = half_outer(inner_rows, grad_ffn)
    grad_inner = half_back(grad_ffn, ffn_down)
    grad_up = (grad_inner * jax.nn.silu(gate_rows)).astype(jnp.bfloat16)
    grad_gate = (grad_inner * up_rows * silu_slope(gate_rows)).astype(jnp.bfloat16)
    ffn_gate_grad = half_outer(hidden_two, grad_gate)
    ffn_up_grad = half_outer(hidden_two, grad_up)
    hidden_two_part = half_back(grad_gate, ffn_gate) + half_back(grad_up, ffn_up)
    hidden_two_part, ffn_gate_grad, ffn_up_grad, ffn_down_grad = lax.optimization_barrier(
        (hidden_two_part, ffn_gate_grad, ffn_up_grad, ffn_down_grad)
    )
    ffn_grads = lax.psum((ffn_gate_grad, ffn_up_grad, ffn_down_grad), "seq")
    grad_hidden_two = head_sum(hidden_two_part, "head", 3)
    ffn_gain_grad = jnp.sum(grad_hidden_two * normed_two, axis=0)
    grad_middle = grad_rows + rms_back(grad_hidden_two * ffn_gain, normed_two, scale_two)
    grad_mixer = grad_middle.astype(jnp.bfloat16)
    out_weight_grad = half_outer(gated_rows, grad_mixer)
    grad_gated = half_back(grad_mixer, out_weight)
    grad_normed = grad_gated * gate_act
    grad_gate_raw = (grad_gated * normed_gain * silu_slope(gate_raw)).astype(jnp.bfloat16)
    head_gain_part = jnp.sum(grad_normed * head_normed, axis=0)
    grad_mixed = rms_back(grad_normed * head_gain, head_normed, head_scale).reshape(
        seq_count, tok_rows, value_size
    )
    state_pull = jnp.einsum("btk,btv->bvk", query_decayed, grad_mixed, precision=HIGH)
    grad_state_out = carried_in(block_decay, state_pull, "seq", True, 1)
    grad_queries, grad_keys, grad_values, grad_decay = gla_backward(
        queries, key_rows, value_rows, grad_mixed, scores, factors, states, prefix, state_in, grad_state_out
    )
    grad_conv_out = jnp.concatenate([grad_queries * factor, grad_keys, grad_values], axis=2)
    grad_conv_pre = grad_conv_out * silu_slope(conv_pre)
    grad_padded = jnp.zeros_like(padded)
    tap_grads = []
    for offset in range(taps):
        grad_padded = grad_padded + jnp.pad(
            conv_weight[offset] * grad_conv_pre, ((0, 0), (offset, taps - 1 - offset), (0, 0))
        )
        tap_grads.append(
            jnp.sum(padded[:, offset : offset + tok_rows] * grad_conv_pre, axis=(0, 1))
        )
    conv_grad = jnp.stack(tap_grads)
    edge_back = shifted(grad_padded[:, : taps - 1], "seq", -1)
    grad_conv_in = grad_padded[:, taps - 1 :] + jnp.pad(
        edge_back, ((0, 0), (tok_rows - taps + 1, 0), (0, 0))
    )
    grad_in_rows = grad_conv_in.reshape(row_count, 2 * key_size + value_size).astype(jnp.bfloat16)
    grad_query_raw = grad_in_rows[:, :key_size]
    grad_key_raw = grad_in_rows[:, key_size : 2 * key_size]
    grad_value_raw = grad_in_rows[:, 2 * key_size :]
    grad_pre = grad_decay.reshape(row_count, key_size) / 16.0 * jax.nn.sigmoid(-decay_pre)
    decay_bias_grad = jnp.sum(grad_pre, axis=0)
    decay_up_grad = exact_outer(rank_rows, grad_pre)
    grad_rank = exact_back(grad_pre, up_wide)
    decay_down_part = exact_outer(hidden_wide, grad_rank)
    query_weight_grad = half_outer(hidden_one, grad_query_raw)
    key_weight_grad = half_outer(hidden_one, grad_key_raw)
    value_weight_grad = half_outer(hidden_one, grad_value_raw)
    gate_weight_grad = half_outer(hidden_one, grad_gate_raw)
    hidden_part = half_back(grad_query_raw, query_weight) + half_back(grad_key_raw, key_weight)
    hidden_part = (
        hidden_part
        + half_back(grad_value_raw, value_weight)
        + half_back(grad_gate_raw, gate_weight)
    )
    hidden_part = hidden_part + exact_back(grad_rank, down_wide)
    down_rows = decay_down_part.size // model_width
    tail_rows = -(-(down_rows + 1) // 32) * 32
    tail = jnp.concatenate([decay_down_part.reshape(-1), head_gain_part])
    tail = jnp.pad(tail, (0, tail_rows * model_width - tail.size)).reshape(tail_rows, model_width)
    summed = head_sum(jnp.concatenate([hidden_part, ffn_part, tail], axis=0), "head", 4)
    grad_hidden_one = summed[:row_count]
    block_output = (middle + summed[row_count : 2 * row_count]).reshape(seq_count, tok_rows, model_width)
    tail = summed[2 * row_count :].reshape(-1)[: decay_down_part.size + head_gain_part.size]
    attn_gain_grad = jnp.sum(grad_hidden_one * normed_one, axis=0)
    input_grad = (
        grad_middle + rms_back(grad_hidden_one * attn_gain, normed_one, scale_one)
    ).reshape(seq_count, tok_rows, model_width)
    small = [tail, attn_gain_grad, ffn_gain_grad, decay_up_grad, decay_bias_grad, conv_grad]
    small_row = jnp.concatenate([item.reshape(-1) for item in small])
    small_rows = -(-small_row.size // (8 * key_size)) * 8
    small_row = jnp.pad(small_row, (0, small_rows * key_size - small_row.size))
    joined = jnp.concatenate([query_weight_grad, small_row.reshape(small_rows, key_size)], axis=0)
    rest = (joined, key_weight_grad, value_weight_grad, gate_weight_grad, out_weight_grad)
    ffn_grads, rest = lax.optimization_barrier((ffn_grads, rest))
    joined, key_weight_grad, value_weight_grad, gate_weight_grad, out_weight_grad = lax.psum(rest, "seq")
    ffn_gate_grad, ffn_up_grad, ffn_down_grad = ffn_grads
    query_weight_grad = joined[:model_width]
    small_row = joined[model_width:].reshape(-1)
    parts, start = [], 0
    for item in [decay_down_part, head_gain_part] + small[1:]:
        parts.append(small_row[start : start + item.size].reshape(item.shape))
        start += item.size
    decay_down_grad, head_gain_grad, attn_gain_grad, ffn_gain_grad, decay_up_grad, decay_bias_grad, conv_grad = parts
    query_conv_grad = conv_grad[:, :key_size]
    key_conv_grad = conv_grad[:, key_size : 2 * key_size]
    value_conv_grad = conv_grad[:, 2 * key_size :]
    return (
        block_output,
        input_grad,
        attn_gain_grad,
        query_weight_grad,
        key_weight_grad,
        value_weight_grad,
        gate_weight_grad,
        decay_down_grad,
        decay_up_grad,
        decay_bias_grad,
        query_conv_grad,
        key_conv_grad,
        value_conv_grad,
        head_gain_grad,
        out_weight_grad,
        ffn_gain_grad,
        ffn_gate_grad,
        ffn_up_grad,
        ffn_down_grad,
    )


def solution(mesh):
    in_specs = (
        P(None, "seq", None),
        P(),
        P(None, "head"),
        P(None, "head"),
        P(None, "head"),
        P(None, "head"),
        P(),
        P(None, "head"),
        P("head"),
        P(None, "head"),
        P(None, "head"),
        P(None, "head"),
        P(),
        P("head", None),
        P(),
        P(None, "head"),
        P(None, "head"),
        P("head", None),
        P(None, "seq", None),
    )
    out_specs = (
        P(None, "seq", None),
        P(None, "seq", None),
        P(),
        P(None, "head"),
        P(None, "head"),
        P(None, "head"),
        P(None, "head"),
        P(),
        P(None, "head"),
        P("head"),
        P(None, "head"),
        P(None, "head"),
        P(None, "head"),
        P(),
        P("head", None),
        P(),
        P(None, "head"),
        P(None, "head"),
        P("head", None),
    )
    return jax.shard_map(shards, mesh=mesh, in_specs=in_specs, out_specs=out_specs, check_vma=False)
```

```python
import functools

import jax
import jax.numpy as jnp
import numpy as np
from jax import lax
from jax.experimental import pallas as pl
from jax.experimental.pallas import tpu as pltpu
from jax.sharding import PartitionSpec as P

EPS = 1e-06
HIGH = lax.Precision.HIGHEST
MESH = pl.DeviceIdType.MESH
QUICK = pl.CostEstimate(flops=1, bytes_accessed=1, transcendentals=0)


def shifted(value, axis, steps):
    count = lax.axis_size(axis)
    initial, last = (max(0, -steps), min(count, count - steps))
    return lax.ppermute(value, axis, [(source, source + steps) for source in range(initial, last)])


def rms_scale(values):
    return lax.rsqrt(jnp.mean(values * values, axis=-1, keepdims=True) + EPS)


def rms_back(grad_normed, normed, scale):
    return scale * (grad_normed - normed * jnp.mean(grad_normed * normed, axis=-1, keepdims=True))


def silu_slope(values):
    sigma = jax.nn.sigmoid(values)
    return sigma * (1.0 + values * (1.0 - sigma))


def half_dot(left, right):
    return jnp.dot(left, right, preferred_element_type=jnp.float32)


def half_outer(left, right):
    return lax.dot_general(
        left, right, (((0,), (0,)), ((), ())), preferred_element_type=jnp.float32
    )


def half_back(left, right):
    return lax.dot_general(
        left, right, (((1,), (1,)), ((), ())), preferred_element_type=jnp.float32
    )


def exact_dot(left, right):
    return jnp.dot(left, right, precision=HIGH, preferred_element_type=jnp.float32)


def exact_outer(left, right):
    return lax.dot_general(
        left, right, (((0,), (0,)), ((), ())), precision=HIGH, preferred_element_type=jnp.float32
    )


def exact_back(left, right):
    return lax.dot_general(
        left, right, (((1,), (1,)), ((), ())), precision=HIGH, preferred_element_type=jnp.float32
    )


def dot3(left, right, dims):
    left_high = left.astype(jnp.bfloat16)
    right_high = right.astype(jnp.bfloat16)
    left_low = (left - left_high.astype(jnp.float32)).astype(jnp.bfloat16)
    right_low = (right - right_high.astype(jnp.float32)).astype(jnp.bfloat16)

    def one(a, b):
        return lax.dot_general(a, b, (dims, ((), ())), preferred_element_type=jnp.float32)

    return one(left_high, right_high) + (one(left_high, right_low) + one(left_low, right_high))


PLAIN = ((1,), (0,))
BACK = ((1,), (1,))
OUTER = ((0,), (0,))


def sum_rows(zero_one, rows):
    first = rows.astype(jnp.bfloat16)
    rest = rows - first.astype(jnp.float32)
    second = rest.astype(jnp.bfloat16)
    third = (rest - second.astype(jnp.float32)).astype(jnp.bfloat16)

    def one(part):
        return jnp.dot(zero_one, part, preferred_element_type=jnp.float32)

    return one(first) + (one(second) + one(third))


def level_tables(size):
    place = np.arange(size)
    spans, masks = [], []
    half = size // 2
    while half >= 1:
        odd = (place // half) % 2 == 1
        edge = np.where(odd, (place // half) * half - 1, (place // half) * half + half - 1)
        column = place[None, :]
        forward = (column > edge[:, None]) & (column <= place[:, None])
        backward = (column > place[:, None]) & (column <= edge[:, None])
        spans.append(np.where(odd[:, None], forward, backward))
        same = (place[:, None] // (2 * half)) == (place[None, :] // (2 * half))
        masks.append(same & (odd[:, None] != odd[None, :]))
        half //= 2
    spans.append(place[None, :] <= place[:, None])
    spans.append(place[None, :] > place[:, None])
    return np.concatenate(spans).astype(np.float32), np.stack(masks).astype(np.float32)


def gla_forward_kernel(
    query, key, value, decay, spans, masks,
    out, query_decayed, scores_out, factors_out, states, prefix, last_state, last_decay,
    state, running,
):
    step = pl.program_id(0)
    seqs, size, width = query.shape
    levels = masks.shape[0]

    @pl.when(step == 0)
    def _():
        state[...] = jnp.zeros_like(state)
        running[...] = jnp.ones_like(running)

    row = lax.broadcasted_iota(jnp.int32, (size, size), 0)
    col = lax.broadcasted_iota(jnp.int32, (size, size), 1)
    row_wide = lax.broadcasted_iota(jnp.int32, (size, width), 0)
    for at in range(seqs):
        q, k, v = query[at], key[at], value[at]
        factors = jnp.exp(sum_rows(spans[...], decay[at]))
        factors_out[at, 0] = factors
        scores = jnp.where(row == col, jnp.sum(q * k, axis=1, keepdims=True), 0.0)
        for level in range(levels):
            half = size >> (level + 1)
            odd = (row_wide // half) % 2 == 1
            mixed = jnp.where(odd, q, k) * factors[level * size : (level + 1) * size]
            pairs = dot3(mixed, mixed, BACK) * masks[level]
            scores = scores + jnp.where(row > col, pairs, 0.0)
        scores_out[at, 0] = scores
        ahead = factors[levels * size : (levels + 1) * size]
        behind = factors[(levels + 1) * size :]
        whole = ahead[size - 1 : size]
        before = state[at]
        states[at, 0] = before
        prior = running[at, 0:1]
        prefix[at, 0] = running[at]
        query_ahead = q * ahead
        query_decayed[at] = query_ahead * prior
        out[at] = dot3(scores, v, PLAIN) + dot3(query_ahead, before, BACK)
        after = before * whole + dot3(v, k * behind, OUTER)
        state[at] = after
        running[at] = running[at] * whole
        last_state[at] = after
        last_decay[at] = running[at]


def gla_backward_kernel(
    query, key, value, grad, scores_in, factors_in, states, prefix, state_in, grad_last, masks, suffix,
    grad_query, grad_key, grad_value, grad_decay,
    grad_state,
):
    step = pl.program_id(0)
    seqs, size, width = query.shape
    levels = masks.shape[0]

    @pl.when(step == 0)
    def _():
        grad_state[...] = grad_last[...]

    row = lax.broadcasted_iota(jnp.int32, (size, size), 0)
    col = lax.broadcasted_iota(jnp.int32, (size, size), 1)
    row_wide = lax.broadcasted_iota(jnp.int32, (size, width), 0)
    for at in range(seqs):
        q, k, v, do = query[at], key[at], value[at], grad[at]
        factors = factors_in[at, 0]
        ahead = factors[levels * size : (levels + 1) * size]
        behind = factors[(levels + 1) * size :]
        whole = ahead[size - 1 : size]
        before = states[at, 0] + state_in[at] * prefix[at, 0, 0:1]
        after_grad = grad_state[at]
        key_behind = k * behind
        after = before * whole + dot3(v, key_behind, OUTER)
        dv = dot3(scores_in[at, 0], do, OUTER) + dot3(key_behind, after_grad, BACK)
        lower = dot3(do, v, BACK)
        both = jnp.where(row >= col, lower, dot3(v, do, BACK))
        diagonal = jnp.sum(do * v, axis=1, keepdims=True)
        dq = dot3(do, before, PLAIN) * ahead
        dk = dot3(v, after_grad, PLAIN) * behind
        for level in range(levels):
            half = size >> (level + 1)
            odd = (row_wide // half) % 2 == 1
            factor = factors[level * size : (level + 1) * size]
            mixed = jnp.where(odd, q, k) * factor
            back = dot3(both * masks[level], mixed, PLAIN) * factor
            dq = dq + jnp.where(odd, back, 0.0)
            dk = dk + jnp.where(odd, 0.0, back)
        carried = jnp.sum(after * after_grad, axis=0, keepdims=True)
        grad_decay[at] = sum_rows(suffix[...], q * dq - k * dk) + carried
        grad_query[at] = dq + diagonal * k
        grad_key[at] = dk + diagonal * q
        grad_value[at] = dv
        grad_state[at] = after_grad * whole + dot3(do, q * ahead, OUTER)


def chunk_of(count):
    size = 128
    while count % size:
        size //= 2
    return size


def gla_forward(query, key, value, decay):
    seqs, count, width = query.shape
    values = value.shape[2]
    size = chunk_of(count)
    chunks = count // size
    spans, masks = level_tables(size)
    tall = spans.shape[0]

    def rows(columns):
        return pl.BlockSpec((seqs, size, columns), lambda i: (0, i, 0))

    def whole(*shape):
        return pl.BlockSpec(shape, lambda i: (0,) * len(shape))

    def chunk(*shape):
        return pl.BlockSpec((seqs, 1) + shape, lambda i: (0, i, 0, 0))

    f32 = jnp.float32
    return pl.pallas_call(
        gla_forward_kernel,
        grid=(chunks,),
        in_specs=[rows(width), rows(width), rows(values), rows(width), whole(*spans.shape), whole(*masks.shape)],
        out_specs=[
            rows(values), rows(width), chunk(size, size), chunk(tall, width),
            chunk(values, width), chunk(8, width), whole(seqs, values, width), whole(seqs, 8, width),
        ],
        out_shape=[
            jax.ShapeDtypeStruct((seqs, count, values), f32),
            jax.ShapeDtypeStruct((seqs, count, width), f32),
            jax.ShapeDtypeStruct((seqs, chunks, size, size), f32),
            jax.ShapeDtypeStruct((seqs, chunks, tall, width), f32),
            jax.ShapeDtypeStruct((seqs, chunks, values, width), f32),
            jax.ShapeDtypeStruct((seqs, chunks, 8, width), f32),
            jax.ShapeDtypeStruct((seqs, values, width), f32),
            jax.ShapeDtypeStruct((seqs, 8, width), f32),
        ],
        scratch_shapes=[pltpu.VMEM((seqs, values, width), f32), pltpu.VMEM((seqs, 8, width), f32)],
        cost_estimate=QUICK,
        compiler_params=pltpu.CompilerParams(vmem_limit_bytes=48 * 1024 * 1024),
        name="gla_local",
    )(query, key, value, decay, jnp.asarray(spans, jnp.bfloat16), jnp.asarray(masks))


def gla_backward(query, key, value, grad, scores, factors, states, prefix, state_in, grad_last):
    seqs, count, width = query.shape
    values = value.shape[2]
    size = chunk_of(count)
    chunks = count // size
    spans, masks = level_tables(size)
    tall = spans.shape[0]
    suffix = np.triu(np.ones((size, size), np.float32))

    def rows(columns):
        return pl.BlockSpec((seqs, size, columns), lambda i: (0, chunks - 1 - i, 0))

    def whole(*shape):
        return pl.BlockSpec(shape, lambda i: (0,) * len(shape))

    def chunk(*shape):
        return pl.BlockSpec((seqs, 1) + shape, lambda i: (0, chunks - 1 - i, 0, 0))

    f32 = jnp.float32
    return pl.pallas_call(
        gla_backward_kernel,
        grid=(chunks,),
        in_specs=[
            rows(width), rows(width), rows(values), rows(values), chunk(size, size), chunk(tall, width),
            chunk(values, width), chunk(8, width), whole(seqs, values, width), whole(seqs, values, width),
            whole(*masks.shape), whole(*suffix.shape),
        ],
        out_specs=[rows(width), rows(width), rows(values), rows(width)],
        out_shape=[
            jax.ShapeDtypeStruct((seqs, count, width), f32),
            jax.ShapeDtypeStruct((seqs, count, width), f32),
            jax.ShapeDtypeStruct((seqs, count, values), f32),
            jax.ShapeDtypeStruct((seqs, count, width), f32),
        ],
        scratch_shapes=[pltpu.VMEM((seqs, values, width), f32)],
        cost_estimate=QUICK,
        compiler_params=pltpu.CompilerParams(vmem_limit_bytes=48 * 1024 * 1024),
        name="gla_back",
    )(query, key, value, grad, scores, factors, states, prefix, state_in, grad_last,
      jnp.asarray(masks), jnp.asarray(suffix, jnp.bfloat16))


def greet(axis, partners):
    barrier = pltpu.get_barrier_semaphore()
    for partner in partners:
        pl.semaphore_signal(barrier, inc=1, device_id={axis: partner}, device_id_type=MESH)
    pl.semaphore_wait(barrier, len(partners))


def prefix_kernel(axis, reverse, block, out, total, received, send_sem, recv_sem):
    steps, seqs, tall, width = total.shape
    values = tall - 8
    me = lax.axis_index(axis)
    uppers = [(me // (1 << step)) % 2 for step in range(steps)]
    partners = [me + (1 << step) * (1 - 2 * upper) for step, upper in enumerate(uppers)]
    greet(axis, partners)
    total[0] = block[...]
    out[...] = jnp.zeros_like(out)
    passed = jnp.ones((seqs, 1, width), jnp.float32)
    for step in range(steps):
        copy = pltpu.make_async_remote_copy(
            src_ref=total.at[step],
            dst_ref=received.at[step],
            send_sem=send_sem.at[step],
            recv_sem=recv_sem.at[step],
            device_id={axis: partners[step]},
            device_id_type=MESH,
        )
        copy.start()
        copy.wait()
        later = uppers[step] == (0 if reverse else 1)
        theirs = received[step, :, :values]
        their_decay = received[step, :, values:]
        out[...] = jnp.where(later, theirs * passed + out[...], out[...])
        passed = jnp.where(later, their_decay[:, 0:1] * passed, passed)
        if step + 1 < steps:
            mine = total[step, :, :values]
            my_decay = total[step, :, values:]
            total[step + 1, :, :values] = jnp.where(
                later, theirs * my_decay[:, 0:1] + mine, mine * their_decay[:, 0:1] + theirs
            )
            total[step + 1, :, values:] = my_decay * their_decay


def carried_in(decay, state, axis, reverse, call_id):
    count = lax.axis_size(axis)
    steps = count.bit_length() - 1
    assert count == 1 << steps
    block = jnp.concatenate([state, decay], axis=1)
    slots = pltpu.VMEM((steps,) + block.shape, jnp.float32)
    return pl.pallas_call(
        functools.partial(prefix_kernel, axis, reverse),
        out_shape=jax.ShapeDtypeStruct(state.shape, jnp.float32),
        in_specs=[pl.BlockSpec(memory_space=pltpu.VMEM)],
        out_specs=pl.BlockSpec(memory_space=pltpu.VMEM),
        scratch_shapes=[slots, slots, pltpu.SemaphoreType.DMA((steps,)), pltpu.SemaphoreType.DMA((steps,))],
        cost_estimate=QUICK,
        compiler_params=pltpu.CompilerParams(
            collective_id=call_id, has_side_effects=True, vmem_limit_bytes=32 * 1024 * 1024
        ),
        name="state_prefix",
    )(block)


def sum_kernel(axis, terms, out, partial, from_near, from_far, send_sem, recv_sem):
    pieces = terms.shape[0]
    me = lax.axis_index(axis)
    low, high = me % 2, me // 2
    near = me + 1 - 2 * low
    far = me + 2 - 4 * high
    mine = 2 * low + high
    other = 2 * low + 1 - high
    greet(axis, [near, far])

    def copy(kind, piece, source, target, device):
        return pltpu.make_async_remote_copy(
            src_ref=source,
            dst_ref=target,
            send_sem=send_sem.at[kind, piece],
            recv_sem=recv_sem.at[kind, piece],
            device_id={axis: device},
            device_id_type=MESH,
        )

    def halves(piece):
        return copy(0, piece, terms.at[piece, pl.ds(2 - 2 * low, 2)], from_near.at[piece], near)

    def quarters(piece):
        return copy(1, piece, partial.at[piece, 1 - high], from_far.at[piece], far)

    def back_far(piece):
        return copy(2, piece, out.at[piece, mine], out.at[piece, mine], far)

    def back_near(piece):
        return copy(3, piece, out.at[piece, mine], out.at[piece, mine], near)

    def pass_near(piece):
        return copy(4, piece, out.at[piece, other], out.at[piece, other], near)

    for piece in range(pieces):
        halves(piece).start()
    for piece in range(pieces):
        halves(piece).wait_recv()
        partial[piece] = terms[piece, pl.ds(2 * low, 2)] + from_near[piece]
        quarters(piece).start()
    for piece in range(pieces):
        quarters(piece).wait_recv()
        out[piece, mine] = partial[piece, high] + from_far[piece]
        back_far(piece).start()
        back_near(piece).start()
    for piece in range(pieces):
        back_far(piece).wait_recv()
        pass_near(piece).start()
    for piece in range(pieces):
        back_near(piece).wait_recv()
        pass_near(piece).wait_recv()
        for made in (halves, quarters, back_far, back_near, pass_near):
            made(piece).wait_send()


def head_sum(terms, axis, call_id):
    rows, columns = terms.shape
    if lax.axis_size(axis) != 4 or rows % 32:
        return lax.psum(terms, axis)
    pieces = next(count for count in (4, 5, 3, 2, 1) if rows % (32 * count) == 0)
    deep = rows // (4 * pieces)
    f32 = jnp.float32
    out = pl.pallas_call(
        functools.partial(sum_kernel, axis),
        out_shape=jax.ShapeDtypeStruct((pieces, 4, deep, columns), f32),
        in_specs=[pl.BlockSpec(memory_space=pltpu.VMEM)],
        out_specs=pl.BlockSpec(memory_space=pltpu.VMEM),
        scratch_shapes=[
            pltpu.VMEM((pieces, 2, deep, columns), f32),
            pltpu.VMEM((pieces, 2, deep, columns), f32),
            pltpu.VMEM((pieces, deep, columns), f32),
            pltpu.SemaphoreType.DMA((5, pieces)),
            pltpu.SemaphoreType.DMA((5, pieces)),
        ],
        cost_estimate=QUICK,
        compiler_params=pltpu.CompilerParams(
            collective_id=call_id, has_side_effects=True, vmem_limit_bytes=48 * 1024 * 1024
        ),
        name="head_sum",
    )(terms.reshape(pieces, 4, deep, columns))
    return out.reshape(rows, columns)


def seq_sum_kernel(axis, terms, out, *scratch):
    pieces, count = terms.shape[:2]
    steps = count.bit_length() - 1
    received, partial = scratch[:steps], scratch[steps : 2 * steps - 1]
    send_sem, recv_sem = scratch[2 * steps - 1 :]
    me = lax.axis_index(axis)
    bits = [(me // (1 << step)) % 2 for step in range(steps)]
    partners = [me + (1 << step) * (1 - 2 * bit) for step, bit in enumerate(bits)]
    starts = [0]
    for step, bit in enumerate(bits):
        starts.append(starts[-1] + bit * (count >> (step + 1)))
    greet(axis, partners)

    def copy(slot, step, piece, source, target):
        return pltpu.make_async_remote_copy(
            src_ref=source,
            dst_ref=target,
            send_sem=send_sem.at[slot, piece],
            recv_sem=recv_sem.at[slot, piece],
            device_id={axis: partners[step]},
            device_id_type=MESH,
        )

    def down(step, piece):
        half = count >> (step + 1)
        held = terms if step == 0 else partial[step - 1]
        return copy(
            step, step, piece, held.at[piece, pl.ds((1 - bits[step]) * half, half)], received[step].at[piece]
        )

    def up(step, piece):
        half = count >> (step + 1)
        place = out.at[piece, pl.ds(starts[step + 1], half)]
        return copy(steps + step, step, piece, place, place)

    for piece in range(pieces):
        down(0, piece).start()
    for step in range(steps):
        half = count >> (step + 1)
        held = terms if step == 0 else partial[step - 1]
        for piece in range(pieces):
            down(step, piece).wait_recv()
            kept = held[piece, pl.ds(bits[step] * half, half)] + received[step][piece]
            if step + 1 < steps:
                partial[step][piece] = kept
                down(step + 1, piece).start()
            else:
                out[piece, pl.ds(starts[steps], 1)] = kept
                up(step, piece).start()
    for step in range(steps - 1, -1, -1):
        for piece in range(pieces):
            up(step, piece).wait_recv()
            if step:
                up(step - 1, piece).start()
    for step in range(steps):
        for piece in range(pieces):
            down(step, piece).wait_send()
            up(step, piece).wait_send()


def seq_sum(terms, axis, call_id, pieces=3):
    rows, columns = terms.shape
    count = lax.axis_size(axis)
    steps = count.bit_length() - 1
    assert count == 1 << steps
    deep = -(-rows // (8 * pieces * count)) * 8
    shape = (pieces, count, deep, columns)
    padded = jnp.pad(terms, ((0, pieces * count * deep - rows), (0, 0)))
    f32 = jnp.float32
    slots = [pltpu.VMEM((pieces, count >> (step + 1), deep, columns), f32) for step in range(steps)]
    out = pl.pallas_call(
        functools.partial(seq_sum_kernel, axis),
        out_shape=jax.ShapeDtypeStruct(shape, f32),
        in_specs=[pl.BlockSpec(memory_space=pltpu.VMEM)],
        out_specs=pl.BlockSpec(memory_space=pltpu.VMEM),
        scratch_shapes=slots
        + slots[: steps - 1]
        + [pltpu.SemaphoreType.DMA((2 * steps, pieces)), pltpu.SemaphoreType.DMA((2 * steps, pieces))],
        cost_estimate=QUICK,
        compiler_params=pltpu.CompilerParams(
            collective_id=call_id, has_side_effects=True, vmem_limit_bytes=48 * 1024 * 1024
        ),
        name="seq_sum",
    )(padded.reshape(shape))
    return out.reshape(pieces * count * deep, columns)[:rows]


def shards(
    block_input,
    attn_gain,
    query_weight,
    key_weight,
    value_weight,
    gate_weight,
    decay_down,
    decay_up,
    decay_bias,
    query_conv,
    key_conv,
    value_conv,
    head_gain,
    out_weight,
    ffn_gain,
    ffn_gate,
    ffn_up,
    ffn_down,
    out_grad,
):
    seq_count, tok_rows, model_width = block_input.shape
    key_size = query_weight.shape[1]
    value_size = value_weight.shape[1]
    taps = query_conv.shape[0]
    row_count = seq_count * tok_rows
    inputs = block_input.reshape(row_count, model_width)
    scale_one = rms_scale(inputs)
    normed_one = inputs * scale_one
    hidden_one = (normed_one * attn_gain).astype(jnp.bfloat16)
    query_raw = half_dot(hidden_one, query_weight)
    key_raw = half_dot(hidden_one, key_weight)
    value_raw = half_dot(hidden_one, value_weight)
    gate_raw = half_dot(hidden_one, gate_weight)
    hidden_wide = hidden_one.astype(jnp.float32)
    down_wide = decay_down.astype(jnp.float32)
    up_wide = decay_up.astype(jnp.float32)
    rank_rows = exact_dot(hidden_wide, down_wide)
    decay_pre = exact_dot(rank_rows, up_wide) + decay_bias
    decay_log = (jax.nn.log_sigmoid(decay_pre) / 16.0).reshape(seq_count, tok_rows, key_size)
    conv_in = jnp.concatenate([query_raw, key_raw, value_raw], axis=1).reshape(
        seq_count, tok_rows, 2 * key_size + value_size
    )
    conv_weight = jnp.concatenate([query_conv, key_conv, value_conv], axis=1)
    edge_rows = shifted(conv_in[:, tok_rows - (taps - 1) :], "seq", 1)
    padded = jnp.concatenate([edge_rows, conv_in], axis=1)
    conv_pre = jnp.zeros_like(conv_in)
    for offset in range(taps):
        conv_pre = conv_pre + conv_weight[offset] * padded[:, offset : offset + tok_rows]
    conv_out = jax.nn.silu(conv_pre)
    factor = key_size ** (-0.5)
    queries = conv_out[:, :, :key_size] * factor
    key_rows = conv_out[:, :, key_size : 2 * key_size]
    value_rows = conv_out[:, :, 2 * key_size :]
    local_out, query_decayed, scores, factors, states, prefix, local_state, block_decay = gla_forward(
        queries, key_rows, value_rows, decay_log
    )
    state_in = carried_in(block_decay, local_state, "seq", False, 0)
    mixed_rows = local_out + jnp.einsum("btk,bvk->btv", query_decayed, state_in, precision=HIGH)
    mixed_rows = mixed_rows.reshape(row_count, value_size)
    head_scale = rms_scale(mixed_rows)
    head_normed = mixed_rows * head_scale
    normed_gain = head_normed * head_gain
    gate_act = jax.nn.silu(gate_raw)
    gated_rows = (normed_gain * gate_act).astype(jnp.bfloat16)
    mixer_out = head_sum(half_dot(gated_rows, out_weight), "head", 2)
    middle = inputs + mixer_out
    scale_two = rms_scale(middle)
    normed_two = middle * scale_two
    hidden_two = (normed_two * ffn_gain).astype(jnp.bfloat16)
    gate_rows = half_dot(hidden_two, ffn_gate)
    up_rows = half_dot(hidden_two, ffn_up)
    inner_rows = (jax.nn.silu(gate_rows) * up_rows).astype(jnp.bfloat16)
    ffn_part = half_dot(inner_rows, ffn_down)
    grad_rows = out_grad.reshape(row_count, model_width)
    grad_ffn = grad_rows.astype(jnp.bfloat16)
    ffn_down_grad = half_outer(inner_rows, grad_ffn)
    grad_inner = half_back(grad_ffn, ffn_down)
    grad_up = (grad_inner * jax.nn.silu(gate_rows)).astype(jnp.bfloat16)
    grad_gate = (grad_inner * up_rows * silu_slope(gate_rows)).astype(jnp.bfloat16)
    ffn_gate_grad = half_outer(hidden_two, grad_gate)
    ffn_up_grad = half_outer(hidden_two, grad_up)
    hidden_two_part = half_back(grad_gate, ffn_gate) + half_back(grad_up, ffn_up)
    hidden_two_part, ffn_gate_grad, ffn_up_grad, ffn_down_grad = lax.optimization_barrier(
        (hidden_two_part, ffn_gate_grad, ffn_up_grad, ffn_down_grad)
    )
    ffn_grads = lax.psum((ffn_gate_grad, ffn_up_grad, ffn_down_grad), "seq")
    grad_hidden_two = head_sum(hidden_two_part, "head", 3)
    ffn_gain_grad = jnp.sum(grad_hidden_two * normed_two, axis=0)
    grad_middle = grad_rows + rms_back(grad_hidden_two * ffn_gain, normed_two, scale_two)
    grad_mixer = grad_middle.astype(jnp.bfloat16)
    out_weight_grad = half_outer(gated_rows, grad_mixer)
    grad_gated = half_back(grad_mixer, out_weight)
    grad_normed = grad_gated * gate_act
    grad_gate_raw = (grad_gated * normed_gain * silu_slope(gate_raw)).astype(jnp.bfloat16)
    head_gain_part = jnp.sum(grad_normed * head_normed, axis=0)
    grad_mixed = rms_back(grad_normed * head_gain, head_normed, head_scale).reshape(
        seq_count, tok_rows, value_size
    )
    state_pull = jnp.einsum("btk,btv->bvk", query_decayed, grad_mixed, precision=HIGH)
    grad_state_out = carried_in(block_decay, state_pull, "seq", True, 1)
    grad_queries, grad_keys, grad_values, grad_decay = gla_backward(
        queries, key_rows, value_rows, grad_mixed, scores, factors, states, prefix, state_in, grad_state_out
    )
    grad_conv_out = jnp.concatenate([grad_queries * factor, grad_keys, grad_values], axis=2)
    grad_conv_pre = grad_conv_out * silu_slope(conv_pre)
    grad_padded = jnp.zeros_like(padded)
    tap_grads = []
    for offset in range(taps):
        grad_padded = grad_padded + jnp.pad(
            conv_weight[offset] * grad_conv_pre, ((0, 0), (offset, taps - 1 - offset), (0, 0))
        )
        tap_grads.append(
            jnp.sum(padded[:, offset : offset + tok_rows] * grad_conv_pre, axis=(0, 1))
        )
    conv_grad = jnp.stack(tap_grads)
    edge_back = shifted(grad_padded[:, : taps - 1], "seq", -1)
    grad_conv_in = grad_padded[:, taps - 1 :] + jnp.pad(
        edge_back, ((0, 0), (tok_rows - taps + 1, 0), (0, 0))
    )
    grad_in_rows = grad_conv_in.reshape(row_count, 2 * key_size + value_size).astype(jnp.bfloat16)
    grad_query_raw = grad_in_rows[:, :key_size]
    grad_key_raw = grad_in_rows[:, key_size : 2 * key_size]
    grad_value_raw = grad_in_rows[:, 2 * key_size :]
    grad_pre = grad_decay.reshape(row_count, key_size) / 16.0 * jax.nn.sigmoid(-decay_pre)
    decay_bias_grad = jnp.sum(grad_pre, axis=0)
    decay_up_grad = exact_outer(rank_rows, grad_pre)
    grad_rank = exact_back(grad_pre, up_wide)
    decay_down_part = exact_outer(hidden_wide, grad_rank)
    query_weight_grad = half_outer(hidden_one, grad_query_raw)
    key_weight_grad = half_outer(hidden_one, grad_key_raw)
    value_weight_grad = half_outer(hidden_one, grad_value_raw)
    gate_weight_grad = half_outer(hidden_one, grad_gate_raw)
    hidden_part = half_back(grad_query_raw, query_weight) + half_back(grad_key_raw, key_weight)
    hidden_part = (
        hidden_part
        + half_back(grad_value_raw, value_weight)
        + half_back(grad_gate_raw, gate_weight)
    )
    hidden_part = hidden_part + exact_back(grad_rank, down_wide)
    down_rows = decay_down_part.size // model_width
    tail_rows = -(-(down_rows + 1) // 32) * 32
    tail = jnp.concatenate([decay_down_part.reshape(-1), head_gain_part])
    tail = jnp.pad(tail, (0, tail_rows * model_width - tail.size)).reshape(tail_rows, model_width)
    summed = head_sum(jnp.concatenate([hidden_part, ffn_part, tail], axis=0), "head", 4)
    grad_hidden_one = summed[:row_count]
    block_output = (middle + summed[row_count : 2 * row_count]).reshape(seq_count, tok_rows, model_width)
    tail = summed[2 * row_count :].reshape(-1)[: decay_down_part.size + head_gain_part.size]
    attn_gain_grad = jnp.sum(grad_hidden_one * normed_one, axis=0)
    input_grad = (
        grad_middle + rms_back(grad_hidden_one * attn_gain, normed_one, scale_one)
    ).reshape(seq_count, tok_rows, model_width)
    small = [tail, attn_gain_grad, ffn_gain_grad, decay_up_grad, decay_bias_grad, conv_grad]
    small_row = jnp.concatenate([item.reshape(-1) for item in small])
    out_side = out_weight_grad.reshape(model_width, -1)
    joined = jnp.concatenate(
        [query_weight_grad, key_weight_grad, value_weight_grad, gate_weight_grad, out_side], axis=1
    )
    wide = joined.shape[1]
    small_rows = -(-small_row.size // wide)
    small_row = jnp.pad(small_row, (0, small_rows * wide - small_row.size))
    joined = jnp.concatenate([joined, small_row.reshape(small_rows, wide)], axis=0)
    joined = seq_sum(joined, "seq", 5)
    ffn_gate_grad, ffn_up_grad, ffn_down_grad = ffn_grads
    query_weight_grad = joined[:model_width, :key_size]
    key_weight_grad = joined[:model_width, key_size : 2 * key_size]
    value_weight_grad = joined[:model_width, 2 * key_size : 2 * key_size + value_size]
    gate_weight_grad = joined[:model_width, 2 * key_size + value_size : 2 * (key_size + value_size)]
    out_weight_grad = joined[:model_width, 2 * (key_size + value_size) :].reshape(out_weight.shape)
    small_row = joined[model_width:].reshape(-1)
    parts, start = [], 0
    for item in [decay_down_part, head_gain_part] + small[1:]:
        parts.append(small_row[start : start + item.size].reshape(item.shape))
        start += item.size
    decay_down_grad, head_gain_grad, attn_gain_grad, ffn_gain_grad, decay_up_grad, decay_bias_grad, conv_grad = parts
    query_conv_grad = conv_grad[:, :key_size]
    key_conv_grad = conv_grad[:, key_size : 2 * key_size]
    value_conv_grad = conv_grad[:, 2 * key_size :]
    return (
        block_output,
        input_grad,
        attn_gain_grad,
        query_weight_grad,
        key_weight_grad,
        value_weight_grad,
        gate_weight_grad,
        decay_down_grad,
        decay_up_grad,
        decay_bias_grad,
        query_conv_grad,
        key_conv_grad,
        value_conv_grad,
        head_gain_grad,
        out_weight_grad,
        ffn_gain_grad,
        ffn_gate_grad,
        ffn_up_grad,
        ffn_down_grad,
    )


def solution(mesh):
    in_specs = (
        P(None, "seq", None),
        P(),
        P(None, "head"),
        P(None, "head"),
        P(None, "head"),
        P(None, "head"),
        P(),
        P(None, "head"),
        P("head"),
        P(None, "head"),
        P(None, "head"),
        P(None, "head"),
        P(),
        P("head", None),
        P(),
        P(None, "head"),
        P(None, "head"),
        P("head", None),
        P(None, "seq", None),
    )
    out_specs = (
        P(None, "seq", None),
        P(None, "seq", None),
        P(),
        P(None, "head"),
        P(None, "head"),
        P(None, "head"),
        P(None, "head"),
        P(),
        P(None, "head"),
        P("head"),
        P(None, "head"),
        P(None, "head"),
        P(None, "head"),
        P(),
        P("head", None),
        P(),
        P(None, "head"),
        P(None, "head"),
        P("head", None),
    )
    return jax.shard_map(shards, mesh=mesh, in_specs=in_specs, out_specs=out_specs, check_vma=False)
```
